32 devices in a mesh: rows: 8 (over z, y), feat: 4 (over x, core).
Axes of the slice: x: 2, y: 2, z: 4, core: 2. Of those that a mesh axis runs over, the one named last changes fastest.
Arguments:
- gradient: float32 [131072], P('rows'), may hold values from -6 to 6
- hessian: bfloat16 [131072], P('rows'), may hold values from 0.049804688 to 1
- groups: int32 [131072], P('rows'), may hold values from 0 to 4095
- leaf_ids: int32 [131072], P('rows'), may hold values from 0 to 31
- bins: int32 [256, 131072], P('feat', 'rows'), may hold values from 0 to 63
- group_sizes: int32 [4096], P('rows'), may hold values from 16 to 63
- variance_ratio: float32 [1], replicated, may hold values from 1 to 16
Outputs:
- histograms: float32 [32, 256, 128], P('rows', 'feat')
- group_means: float32 [4096], P('rows')
The draws below stay inside these ranges and needn't reach their ends.
All inputs are finite; a program needn't handle non-finite values.
Results may differ from the reference program's by a relative error of at most 0.00038.
Values sent between devices are 32-bit elements; how exact they have to be, the bound alone decides.
No kernel may reach another device: no remote copies, remote signals or barrier semaphores. Data moves between devices by JAX's collectives and lax.ppermute only.
A program may use at most 64 MiB of HBM per device.

```python
import math
import jax
import jax.numpy as jnp
import numpy as np
from jax import lax

F = 256
BINS = 64
LEAVES = 32
ROWS = 131072
GROUPS = 4096


def set_ends(drawn, key, low, high):
    longest = drawn.shape.index(max(drawn.shape))
    spots = []
    for shift in (0, 1):
        where = [jax.random.randint(jax.random.fold_in(key, axis), (), 0, length) for axis, length in enumerate(drawn.shape)]
        where[longest] = (where[longest] + shift) % drawn.shape[longest]
        spots.append(tuple(where))
    return drawn.at[spots[0]].set(low).at[spots[1]].set(high)


def block_scale(own_key, shape, pieces, low, top_value):
    level, own = 1.0, jax.random.fold_in(own_key, 6)
    for dim, parts in pieces:
        steps = jnp.exp(jax.random.uniform(jax.random.fold_in(own, dim), (parts,), jnp.float32, low / len(pieces), top_value / len(pieces)))
        level = level * jnp.repeat(steps, shape[dim] // parts).reshape([-1 if axis == dim else 1 for axis in range(len(shape))])
    return level


def rank_bounds(amount, lean):
    weights = [(1 << 20) // math.isqrt(grade ** lean) + 1 for grade in range(1, amount + 1)]
    deviation = 1 + sum(weights) // (1 << 30)
    return np.cumsum(np.array([max(1, weight // deviation) for weight in weights]))


def ranked_ids(rng, shape, count, slope):
    grid = rank_bounds(count, slope)
    ticket = jax.random.randint(jax.random.fold_in(rng, 1), shape, 0, int(grid[count - 1]))
    rank = jnp.searchsorted(jnp.asarray(grid, jnp.int32), ticket, side="right")
    return jax.random.permutation(jax.random.fold_in(rng, 2), count)[rank].astype(jnp.int32)


def bell_draw(own_key, shape, spread, most, cuts=(), kind=jnp.bfloat16):
    level = block_scale(own_key, shape, cuts, -0.22, 0.18) if cuts else 1.0
    drawn = jax.random.normal(own_key, shape, jnp.float32) * spread * level
    return jnp.minimum(jnp.maximum(drawn, -most), most).astype(kind)


def setup_inputs(seed: int = 0) -> dict:
    key_of = jax.random.split(jax.random.key(seed), 8)
    return {
        "gradient": bell_draw(key_of[0], (ROWS,), 1.0, 6.0, ((0, 8),), jnp.float32),
        "hessian": jnp.clip(0.049804688 + 0.9501953 * jax.random.uniform(key_of[1], (ROWS,), jnp.float32) ** block_scale(key_of[1], (ROWS,), ((0, 8),), -0.2, 0.2), 0.049804688, 1.0).astype(jnp.bfloat16),
        "groups": set_ends(ranked_ids(key_of[2], (ROWS,), GROUPS, 1), jax.random.fold_in(key_of[2], 3), 0, GROUPS - 1).astype(jnp.int32),
        "leaf_ids": set_ends(jax.random.randint(key_of[3], (ROWS,), 0, LEAVES), jax.random.fold_in(key_of[3], 1), 0, LEAVES - 1).astype(jnp.int32),
        "bins": set_ends(jax.random.randint(key_of[4], (F, ROWS), 0, BINS), jax.random.fold_in(key_of[4], 1), 0, BINS - 1).astype(jnp.int32),
        "group_sizes": set_ends(jax.random.randint(key_of[5], (GROUPS,), 16, 64), jax.random.fold_in(key_of[5], 1), 16, 63).astype(jnp.int32),
        "variance_ratio": jnp.clip(jnp.exp(jax.random.uniform(key_of[6], (1,), jnp.float32, math.log(1.0), math.log(16.0))), 1.0, 16.0),
    }


def reference(gradient, hessian, groups, leaf_ids, bins, group_sizes, variance_ratio):
    group_total = jax.ops.segment_sum(gradient, groups, num_segments=GROUPS)
    group_means = -group_total / (group_sizes.astype(jnp.float32) + variance_ratio[0])
    adjusted = (gradient + hessian.astype(jnp.float32) * group_means[groups]).astype(jnp.bfloat16)
    weights = jnp.stack([adjusted.astype(jnp.float32), hessian.astype(jnp.float32)], axis=1)

    def one_feature(column):
        index = (leaf_ids * BINS + column).astype(jnp.int32)
        return jax.ops.segment_sum(weights, index, num_segments=LEAVES * BINS)

    per_feature = lax.map(one_feature, bins)
    histograms = per_feature.reshape(F, LEAVES, BINS, 2).transpose(1, 0, 3, 2).reshape(LEAVES, F, 2 * BINS)
    return histograms, group_means
```

```python
import functools

import jax
import jax.numpy as jnp
from jax import lax
from jax.experimental import pallas as pl
from jax.experimental.pallas import tpu as pltpu
from jax.sharding import PartitionSpec as P

BINS = 64
LEAVES = 32
LANES = 128
F8 = jnp.float8_e4m3fn
PARAMS = pltpu.CompilerParams(vmem_limit_bytes=48 * 2**20)


def group_sum_kernel(gradient, groups, sizes, message):
    blocks = gradient.shape[0]
    high_count = message.shape[0] // 2
    own = sizes.shape[0]
    me = lax.axis_index("rows")
    exact = gradient[...]
    first = exact.astype(jnp.bfloat16).astype(jnp.float32)
    rest = exact - first
    second = rest.astype(jnp.bfloat16).astype(jnp.float32)
    third = rest - second
    ids = groups[...]
    high, low = lax.shift_right_logical(ids, 7), ids & (LANES - 1)
    high_levels = lax.broadcasted_iota(jnp.int32, (high_count, LANES), 0)
    low_levels = lax.broadcasted_iota(jnp.int32, (LANES, LANES), 0)
    total = jnp.zeros((3 * high_count, LANES), jnp.float32)
    step = min(32, blocks)
    for start in range(0, blocks, step):
        left, right = [], []
        for j in range(start, start + step):
            here = high[j : j + 1] == high_levels
            left.append(
                jnp.concatenate(
                    [jnp.where(here, part[j : j + 1], 0.0) for part in (first, second, third)], 0
                ).astype(jnp.bfloat16)
            )
            right.append(jnp.where(low[j : j + 1] == low_levels, 1.0, 0.0).astype(jnp.bfloat16))
        total += lax.dot_general(
            jnp.concatenate(left, 1),
            jnp.concatenate(right, 1),
            (((1,), (1,)), ((), ())),
            preferred_element_type=jnp.float32,
        )
    message[:high_count] = (
        total[:high_count] + (total[high_count : 2 * high_count] + total[2 * high_count :])
    )
    own_sizes = sizes[...].astype(jnp.float32)
    for owner in range(high_count // own):
        begin = high_count + owner * own
        message[begin : begin + own] = jnp.where(me == owner, own_sizes, 0.0)


def turn_kernel(bins, turned):
    features, rows = bins.shape
    copies = LANES // features
    levels = BINS // copies
    for start in range(0, rows, LANES):
        block = bins[:, start : start + LANES]
        stack = jnp.concatenate([block - p * levels for p in range(copies)], 0)
        turned[start : start + LANES] = stack.T.astype(jnp.int8)


def weigh_kernel(owner_order, message, ratio, gradient, hessian, groups, leaf_ids, left, unscale):
    blocks = gradient.shape[0]
    high_count = message.shape[0] // 2
    me = lax.axis_index("rows")
    owners = len(owner_order)
    share = LEAVES // owners
    means = -message[:high_count] / (message[high_count:] + ratio[0])
    ids = groups[...]
    high, low = lax.shift_right_logical(ids, 7), ids & (LANES - 1)
    found = []
    for j in range(0, blocks, 8):
        low_here, high_here = low[j : j + 8], high[j : j + 8]
        value = jnp.zeros((8, LANES), jnp.float32)
        for h in range(high_count):
            row = jnp.broadcast_to(means[h : h + 1], (8, LANES))
            picked = jnp.take_along_axis(row, low_here, axis=1, mode="promise_in_bounds")
            value = jnp.where(high_here == h, picked, value)
        found.append(value)
    row_means = jnp.concatenate(found, 0)
    curve = hessian[...].astype(jnp.float32)
    adjusted = (gradient[...] + curve * row_means).astype(jnp.bfloat16).astype(jnp.float32)

    level = jnp.max(jnp.abs(adjusted)) * 32.0
    scale, back = jnp.float32(32.0), jnp.float32(1.0 / 32.0)
    for power in (16, 8, 4, 2, 1):
        big = level > 256.0 * 2.0 ** (power - 1)
        level = jnp.where(big, level * 2.0**-power, level)
        scale = jnp.where(big, scale * 2.0**-power, scale)
        back = jnp.where(big, back * 2.0**power, back)
    unscale[...] = jnp.full(unscale.shape, back, jnp.float32)

    scaled = adjusted * scale
    adjusted_high = scaled.astype(F8).astype(jnp.float32)
    adjusted_low = (scaled - adjusted_high) * 16.0
    curve_high = curve.astype(F8).astype(jnp.float32)
    curve_low = (curve - curve_high) * 16.0

    half = 2 * LEAVES
    row = lax.broadcasted_iota(jnp.int32, (half, LANES), 0)
    place = row // (2 * share)
    owner = jnp.zeros_like(place)
    for position, other in enumerate(owner_order):
        owner = jnp.where(place == position, other, owner)
    leaf_of = (owner ^ me) * share + (row % (2 * share)) // 2
    is_gradient = row % 2 == 0
    leaves = leaf_ids[...]
    for j in range(blocks):
        member = leaves[j : j + 1] == leaf_of
        parts = []
        for one, two in ((adjusted_high, curve_high), (adjusted_low, curve_low)):
            both = jnp.where(is_gradient, one[j : j + 1], two[j : j + 1])
            parts.append(jnp.where(member, both, 0.0))
        left[:, j * LANES : (j + 1) * LANES] = jnp.concatenate(parts, 0).astype(F8)


def histogram_kernel(first_level, level_step, turned, left, unscale, keep, send):
    base = first_level + pl.program_id(0) * level_step
    bins = turned[...]
    hot = []
    for q in range(level_step):
        level = (base + q).astype(jnp.int8)
        hot.append(jnp.where(bins == level, jnp.ones((), F8), jnp.zeros((), F8)))
    both = jnp.dot(left[...], jnp.concatenate(hot, 1), preferred_element_type=jnp.float32)
    half = both.shape[0] // 2
    total = both[:half] + both[half:] * 0.0625
    is_gradient = lax.broadcasted_iota(jnp.int32, (half, 1), 0) % 2 == 0
    total = total * jnp.where(is_gradient, unscale[0:1, 0:1], 1.0)
    keep[...] = total[: half // 2]
    send[...] = total[half // 2 :]


def arrange_kernel(own, histograms):
    share, features, _ = histograms.shape
    copies = LANES // features
    levels = BINS // copies
    for l in range(share):
        rows = []
        for channel in range(2):
            r = 2 * l + channel
            block = jnp.concatenate(
                [own[r : r + 1, kk * LANES : (kk + 1) * LANES] for kk in range(levels)], 0
            )
            for p in range(copies):
                rows.append(block if p == 0 else jnp.roll(block, -p * features, axis=1))
        histograms[l] = jnp.concatenate(rows, 0).T[:features]


def exchange(value, axis, bit):
    count = lax.axis_size(axis)
    return lax.ppermute(value, axis, [(i, i ^ bit) for i in range(count)])


def shards(gradient, hessian, groups, leaf_ids, bins, group_sizes, variance_ratio):
    owners = lax.axis_size("rows")
    bits = [1 << n for n in range(owners.bit_length() - 1)]
    own_groups = group_sizes.shape[0]
    group_count = own_groups * owners
    features, row_count = bins.shape
    blocks = row_count // LANES
    copies = LANES // features
    levels = BINS // copies
    share = LEAVES // owners
    high_count = group_count // LANES
    vmem = pl.BlockSpec(memory_space=pltpu.VMEM)
    smem = pl.BlockSpec(memory_space=pltpu.SMEM)

    gradient = gradient.reshape(blocks, LANES)
    groups = groups.reshape(blocks, LANES)
    leaf_ids = leaf_ids.reshape(blocks, LANES)
    curve = hessian.astype(jnp.float32).reshape(blocks, LANES)

    message = pl.pallas_call(
        group_sum_kernel,
        out_shape=jax.ShapeDtypeStruct((2 * high_count, LANES), jnp.float32),
        in_specs=[vmem] * 3,
        out_specs=vmem,
        compiler_params=PARAMS,
        name="group_sum",
    )(gradient, groups, group_sizes.reshape(own_groups // LANES, LANES))

    turn_rows = min(2048, row_count)
    turned = pl.pallas_call(
        turn_kernel,
        grid=(row_count // turn_rows,),
        out_shape=jax.ShapeDtypeStruct((row_count, LANES), jnp.int8),
        in_specs=[pl.BlockSpec((features, turn_rows), lambda i: (0, i))],
        out_specs=pl.BlockSpec((turn_rows, LANES), lambda i: (i, 0)),
        compiler_params=PARAMS,
        name="turn_bins",
    )(bins)

    for bit in bits:
        message = message + exchange(message, "rows", bit)

    own_rows = own_groups // LANES
    begin = lax.axis_index("rows") * own_rows
    own_total = lax.dynamic_slice_in_dim(message, begin, own_rows, 0)
    own_size = lax.dynamic_slice_in_dim(message, high_count + begin, own_rows, 0)
    own_means = (-own_total / (own_size + variance_ratio[0])).reshape(own_groups)

    owner_order = [0]
    for bit in reversed(bits):
        owner_order = owner_order + [o | bit for o in owner_order]
    left, unscale = pl.pallas_call(
        functools.partial(weigh_kernel, owner_order),
        out_shape=(
            jax.ShapeDtypeStruct((4 * LEAVES, row_count), F8),
            jax.ShapeDtypeStruct((8, LANES), jnp.float32),
        ),
        in_specs=[vmem, smem, vmem, vmem, vmem, vmem],
        out_specs=(vmem, vmem),
        compiler_params=PARAMS,
        name="weigh_rows",
    )(message, variance_ratio, gradient, curve, groups, leaf_ids)

    level_step = 4
    chunks = 2
    chunk_levels = levels // chunks
    pieces = []
    for c in range(chunks):
        keep, send = pl.pallas_call(
            functools.partial(histogram_kernel, c * chunk_levels, level_step),
            grid=(chunk_levels // level_step,),
            out_shape=[jax.ShapeDtypeStruct((LEAVES, chunk_levels * LANES), jnp.float32)] * 2,
            in_specs=[
                pl.BlockSpec((row_count, LANES), lambda i: (0, 0)),
                pl.BlockSpec((4 * LEAVES, row_count), lambda i: (0, 0)),
                pl.BlockSpec((8, LANES), lambda i: (0, 0)),
            ],
            out_specs=[pl.BlockSpec((LEAVES, level_step * LANES), lambda i: (0, i))] * 2,
            compiler_params=PARAMS,
            name="histogram",
        )(turned, left, unscale)
        pieces.append((keep, send))
    done = []
    for keep, send in pieces:
        for n, bit in enumerate(bits):
            total = keep + exchange(send, "rows", bit)
            middle = total.shape[0] // 2
            keep, send = total[:middle], total[middle:]
        done.append(total)

    own = jnp.concatenate(done, 1)
    histograms = pl.pallas_call(
        arrange_kernel,
        out_shape=jax.ShapeDtypeStruct((share, features, 2 * BINS), jnp.float32),
        in_specs=[vmem],
        out_specs=vmem,
        compiler_params=PARAMS,
        name="arrange",
    )(own)
    return histograms, own_means


def solution(mesh):
    in_specs = (P("rows"), P("rows"), P("rows"), P("rows"), P("feat", "rows"), P("rows"), P())
    out_specs = (P("rows", "feat", None), P("rows"))
    return jax.shard_map(shards, mesh=mesh, in_specs=in_specs, out_specs=out_specs, check_vma=False)
```

```python
import functools
import math

import jax
import jax.numpy as jnp
from jax import lax
from jax.experimental import pallas as pl
from jax.experimental.pallas import tpu as pltpu
from jax.sharding import PartitionSpec as P

BINS = 64
LEAVES = 32
LANES = 128
TERMS = 6
TGRANT = 48
K1_STEP = 32
GRANT = 60
WEIGHT = 8
CHUNKS = 2
F8 = jnp.float8_e4m3fn
STREAM = pltpu.CompilerParams(vmem_limit_bytes=int(GRANT * 2**20))
PARAMS = pltpu.CompilerParams(vmem_limit_bytes=48 * 2**20)


def group_sum_kernel(gradient, groups, sizes, message):
    blocks = gradient.shape[0]
    own = sizes.shape[0]
    high_count = message.shape[0] - own
    rest, parts = gradient[...], []
    for n in range(TERMS):
        part = rest.astype(F8).astype(jnp.float32)
        rest = (rest - part) * 16.0
        parts.append(part)
    ids = groups[...]
    high, low = lax.shift_right_logical(ids, 7), ids & (LANES - 1)
    high_levels = lax.broadcasted_iota(jnp.int32, (high_count, LANES), 0).astype(jnp.int8)
    low_levels = lax.broadcasted_iota(jnp.int32, (LANES, LANES), 0).astype(jnp.int8)
    zero, one = jnp.zeros((), F8), jnp.ones((), F8)

    def spread(values, j, rows, dtype):
        return jnp.broadcast_to(values[j : j + 1], (rows, LANES)).astype(dtype)

    total = jnp.zeros((TERMS * high_count, LANES), jnp.float32)
    step = min(K1_STEP, blocks)
    for start in range(0, blocks, step):
        left, right = [], []
        for j in range(start, start + step):
            here = spread(high, j, high_count, jnp.int8) == high_levels
            left.append(
                jnp.concatenate(
                    [jnp.where(here, spread(part, j, high_count, F8), zero) for part in parts], 0
                )
            )
            right.append(jnp.where(spread(low, j, LANES, jnp.int8) == low_levels, one, zero))
        total += lax.dot_general(
            jnp.concatenate(left, 1),
            jnp.concatenate(right, 1),
            (((1,), (1,)), ((), ())),
            preferred_element_type=jnp.float32,
        )
    result = total[(TERMS - 1) * high_count :]
    for n in reversed(range(TERMS - 1)):
        result = result * 0.0625 + total[n * high_count : (n + 1) * high_count]
    message[:high_count] = result
    message[high_count:] = sizes[...].astype(jnp.float32)


def turn_kernel(bins, turned):
    features, rows = bins.shape
    copies = LANES // features
    levels = BINS // copies
    for start in range(0, rows, LANES):
        block = bins[:, start : start + LANES]
        stack = jnp.concatenate([block - p * levels for p in range(copies)], 0)
        turned[start : start + LANES] = stack.astype(jnp.int8).T


def weigh_kernel(owner_order, message, ratio, gradient, hessian, groups, leaf_ids, left, unscale):
    blocks = gradient.shape[0]
    high_count = message.shape[0] // 2
    me = lax.axis_index("rows")
    owners = len(owner_order)
    share = LEAVES // owners
    own = high_count // owners
    size_of = jnp.concatenate(
        [message[pl.ds(high_count + (me ^ o) * own, own)] for o in range(owners)], 0
    )
    means = -message[:high_count] / (size_of + ratio[0])
    ids = groups[...]
    high, low = lax.shift_right_logical(ids, 7), ids & (LANES - 1)
    found = []
    for j in range(0, blocks, 8):
        low_here, high_here = low[j : j + 8], high[j : j + 8]
        value = jnp.zeros((8, LANES), jnp.float32)
        for h in range(high_count):
            row = jnp.broadcast_to(means[h : h + 1], (8, LANES))
            picked = jnp.take_along_axis(row, low_here, axis=1, mode="promise_in_bounds")
            value = jnp.where(high_here == h, picked, value)
        found.append(value)
    row_means = jnp.concatenate(found, 0)
    curve = hessian[...].astype(jnp.float32)
    adjusted = (gradient[...] + curve * row_means).astype(jnp.bfloat16).astype(jnp.float32)

    level = jnp.max(jnp.abs(adjusted)) * 32.0
    scale, back = jnp.float32(32.0), jnp.float32(1.0 / 32.0)
    for power in (16, 8, 4, 2, 1):
        big = level > 256.0 * 2.0 ** (power - 1)
        level = jnp.where(big, level * 2.0**-power, level)
        scale = jnp.where(big, scale * 2.0**-power, scale)
        back = jnp.where(big, back * 2.0**power, back)
    unscale[...] = jnp.full(unscale.shape, back, jnp.float32)

    scaled = adjusted * scale
    adjusted_high = scaled.astype(F8).astype(jnp.float32)
    adjusted_low = (scaled - adjusted_high) * 16.0
    curve_high = curve.astype(F8).astype(jnp.float32)
    curve_low = (curve - curve_high) * 16.0

    half = 2 * LEAVES
    row = lax.broadcasted_iota(jnp.int32, (half, LANES), 0)
    place = row // (2 * share)
    owner = jnp.zeros_like(place)
    for position, other in enumerate(owner_order):
        owner = jnp.where(place == position, other, owner)
    leaf_of = (owner ^ me) * share + (row % (2 * share)) // 2
    leaf_of = leaf_of.astype(jnp.int8)
    is_gradient = (row[:LEAVES] % 2).astype(jnp.int8) == jnp.zeros((), jnp.int8)
    leaves = leaf_ids[...]
    zero = jnp.zeros((), F8)

    def spread(values, j, dtype):
        return jnp.broadcast_to(values[j : j + 1], (LEAVES, LANES)).astype(dtype)

    for j in range(blocks):
        leaf = spread(leaves, j, jnp.int8)
        members = [leaf == leaf_of[:LEAVES], leaf == leaf_of[LEAVES:]]
        parts = []
        for one, two in ((adjusted_high, curve_high), (adjusted_low, curve_low)):
            both = jnp.where(is_gradient, spread(one, j, F8), spread(two, j, F8))
            parts += [jnp.where(member, both, zero) for member in members]
        left[:, j * LANES : (j + 1) * LANES] = jnp.concatenate(parts, 0)


def histogram_kernel(level_step, turned, left, unscale, keep, send):
    base = pl.program_id(0) * level_step
    bins = turned[...]
    hot = []
    for q in range(level_step):
        level = (base + q).astype(jnp.int8)
        hot.append(jnp.where(bins == level, jnp.ones((), F8), jnp.zeros((), F8)))
    both = jnp.dot(left[...], jnp.concatenate(hot, 1), preferred_element_type=jnp.float32)
    half = both.shape[0] // 2
    total = both[:half] + both[half:] * 0.0625
    is_gradient = lax.broadcasted_iota(jnp.int32, (half, 1), 0) % 2 == 0
    total = total * jnp.where(is_gradient, unscale[0:1, 0:1], 1.0)
    keep[...] = total[: half // 2]
    send[...] = total[half // 2 :]


def arrange_kernel(*refs):
    *parts, histograms = refs
    share, features, _ = histograms.shape
    width = features // len(parts)
    copies = LANES // width
    levels = BINS // copies
    for c, own in enumerate(parts):
        for l in range(share):
            rows = []
            for channel in range(2):
                r = 2 * l + channel
                block = jnp.concatenate(
                    [own[r : r + 1, kk * LANES : (kk + 1) * LANES] for kk in range(levels)], 0
                )
                for p in range(copies):
                    rows.append(block if p == 0 else jnp.roll(block, -p * width, axis=1))
            histograms[l, c * width : (c + 1) * width] = jnp.concatenate(rows, 0).T[:width]


def exchange(value, axis, bit):
    count = lax.axis_size(axis)
    return lax.ppermute(value, axis, [(i, i ^ bit) for i in range(count)])


def shards(gradient, hessian, groups, leaf_ids, bins, group_sizes, variance_ratio):
    owners = lax.axis_size("rows")
    bits = [1 << n for n in range(owners.bit_length() - 1)]
    own_groups = group_sizes.shape[0]
    group_count = own_groups * owners
    features, row_count = bins.shape
    blocks = row_count // LANES
    width = features // CHUNKS
    copies = LANES // width
    levels = BINS // copies
    share = LEAVES // owners
    high_count = group_count // LANES
    vmem = pl.BlockSpec(memory_space=pltpu.VMEM)
    smem = pl.BlockSpec(memory_space=pltpu.SMEM)

    gradient = gradient.reshape(blocks, LANES)
    groups = groups.reshape(blocks, LANES)
    leaf_ids = leaf_ids.reshape(blocks, LANES)
    curve = hessian.astype(jnp.float32).reshape(blocks, LANES)

    whole = lambda array: pl.BlockSpec(array.shape, lambda i: (0,) * array.ndim)
    own_rows = own_groups // LANES
    sizes = group_sizes.reshape(own_rows, LANES)
    message = pl.pallas_call(
        group_sum_kernel,
        grid=(1,),
        out_shape=jax.ShapeDtypeStruct((high_count + own_rows, LANES), jnp.float32),
        in_specs=[whole(gradient), whole(groups), whole(sizes)],
        out_specs=vmem,
        compiler_params=STREAM,
        name="group_sum",
    )(gradient, groups, sizes)

    def turn(bins):
        return pl.pallas_call(
            turn_kernel,
            out_shape=jax.ShapeDtypeStruct((row_count, LANES), jnp.int8),
            in_specs=[vmem],
            out_specs=vmem,
            compiler_params=pltpu.CompilerParams(vmem_limit_bytes=TGRANT * 2**20),
            cost_estimate=pl.CostEstimate(flops=0, bytes_accessed=4 * bins.size, transcendentals=0),
            name="turn_bins",
        )(bins)

    turned = []
    for n, bit in enumerate(bits):
        other = exchange(message, "rows", bit)
        if n < CHUNKS:
            turned.append(turn(bins[n * width : (n + 1) * width]))
        totals = message[:high_count] + other[:high_count]
        message = jnp.concatenate([totals, message[high_count:], other[high_count:]], 0)
        if n < CHUNKS:
            message, bins, turned = lax.optimization_barrier((message, bins, turned))

    own_total = lax.dynamic_slice_in_dim(message, lax.axis_index("rows") * own_rows, own_rows, 0)
    own_size = message[high_count : high_count + own_rows]
    own_means = (-own_total / (own_size + variance_ratio[0])).reshape(own_groups)

    owner_order = [0]
    for bit in reversed(bits):
        owner_order = owner_order + [o | bit for o in owner_order]
    left, unscale = pl.pallas_call(
        functools.partial(weigh_kernel, owner_order),
        out_shape=(
            jax.ShapeDtypeStruct((4 * LEAVES, row_count), F8),
            jax.ShapeDtypeStruct((8, LANES), jnp.float32),
        ),
        in_specs=[vmem, smem, vmem, vmem, vmem, vmem],
        out_specs=(vmem, vmem),
        compiler_params=PARAMS,
        name="weigh_rows",
    )(message, variance_ratio, gradient, curve, groups, leaf_ids)

    level_step = math.gcd(levels, 4)
    pieces = []
    for part in turned:
        pieces.append(
            pl.pallas_call(
                functools.partial(histogram_kernel, level_step),
                grid=(levels // level_step,),
                out_shape=[jax.ShapeDtypeStruct((LEAVES, levels * LANES), jnp.float32)] * 2,
                in_specs=[whole(part), whole(left), whole(unscale)],
                out_specs=[pl.BlockSpec((LEAVES, level_step * LANES), lambda i: (0, i))] * 2,
                compiler_params=PARAMS,
                cost_estimate=pl.CostEstimate(
                    flops=WEIGHT * LEAVES * levels * LANES * row_count, bytes_accessed=0, transcendentals=0
                ),
                name="histogram",
            )(part, left, unscale)
        )
    done = []
    for keep, send in pieces:
        for bit in bits:
            total = keep + exchange(send, "rows", bit)
            middle = total.shape[0] // 2
            keep, send = total[:middle], total[middle:]
        done.append(total)

    histograms = pl.pallas_call(
        arrange_kernel,
        out_shape=jax.ShapeDtypeStruct((share, features, 2 * BINS), jnp.float32),
        in_specs=[vmem] * len(done),
        out_specs=vmem,
        compiler_params=PARAMS,
        name="arrange",
    )(*done)
    return histograms, own_means


def solution(mesh):
    in_specs = (P("rows"), P("rows"), P("rows"), P("rows"), P("feat", "rows"), P("rows"), P())
    out_specs = (P("rows", "feat", None), P("rows"))
    return jax.shard_map(shards, mesh=mesh, in_specs=in_specs, out_specs=out_specs, check_vma=False)
```

```python
import functools
import math

import jax
import jax.numpy as jnp
from jax import lax
from jax.experimental import pallas as pl
from jax.experimental.pallas import tpu as pltpu
from jax.sharding import PartitionSpec as P

BINS = 64
LEAVES = 32
LANES = 128
CHUNKS = 2
CROWDED = 16.0
F8 = jnp.float8_e4m3fn
STREAM = pltpu.CompilerParams(vmem_limit_bytes=60 * 2**20)
PARAMS = pltpu.CompilerParams(vmem_limit_bytes=48 * 2**20)


def group_sum_kernel(gradient, groups, sizes, message):
    blocks = gradient.shape[0]
    own = sizes.shape[0]
    high_count = message.shape[0] - own
    exact = gradient[...]
    first = exact.astype(jnp.bfloat16).astype(jnp.float32)
    rest = exact - first
    second = rest.astype(jnp.bfloat16).astype(jnp.float32)
    parts = (first, second, rest - second)
    ids = groups[...]
    high, low = lax.shift_right_logical(ids, 7), ids & (LANES - 1)
    high_levels = lax.broadcasted_iota(jnp.int32, (high_count, LANES), 0).astype(jnp.int16)
    low_levels = lax.broadcasted_iota(jnp.int32, (LANES, LANES), 0).astype(jnp.int16)
    zero, one = jnp.zeros((), jnp.bfloat16), jnp.ones((), jnp.bfloat16)

    def spread(values, j, rows, dtype):
        return jnp.broadcast_to(values[j : j + 1], (rows, LANES)).astype(dtype)

    total = jnp.zeros((3 * high_count, LANES), jnp.float32)
    step = min(32, blocks)
    for start in range(0, blocks, step):
        left, right = [], []
        for j in range(start, start + step):
            here = spread(high, j, high_count, jnp.int16) == high_levels
            left.append(
                jnp.concatenate(
                    [jnp.where(here, spread(part, j, high_count, jnp.bfloat16), zero) for part in parts],
                    0,
                )
            )
            right.append(jnp.where(spread(low, j, LANES, jnp.int16) == low_levels, one, zero))
        total += lax.dot_general(
            jnp.concatenate(left, 1),
            jnp.concatenate(right, 1),
            (((1,), (1,)), ((), ())),
            preferred_element_type=jnp.float32,
        )
    message[:high_count] = (
        total[:high_count] + (total[high_count : 2 * high_count] + total[2 * high_count :])
    )
    message[high_count:] = sizes[...].astype(jnp.float32)


def turn_kernel(bins, turned):
    features, rows = bins.shape
    copies = LANES // features
    levels = BINS // copies
    for start in range(0, rows, LANES):
        block = bins[:, start : start + LANES]
        stack = jnp.concatenate([block - p * levels for p in range(copies)], 0)
        turned[start : start + LANES] = stack.astype(jnp.int8).T


def weigh_kernel(owner_order, message, ratio, gradient, hessian, groups, leaf_ids, left, unscale):
    blocks = gradient.shape[0]
    high_count = message.shape[0] // 2
    me = lax.axis_index("rows")
    owners = len(owner_order)
    share = LEAVES // owners
    own = high_count // owners
    size_of = jnp.concatenate(
        [message[pl.ds(high_count + (me ^ o) * own, own)] for o in range(owners)], 0
    )
    means = -message[:high_count] / (size_of + ratio[0])
    ids = groups[...]
    high, low = lax.shift_right_logical(ids, 7), ids & (LANES - 1)
    found = []
    for j in range(0, blocks, 8):
        low_here, high_here = low[j : j + 8], high[j : j + 8]
        value = jnp.zeros((8, LANES), jnp.float32)
        for h in range(high_count):
            row = jnp.broadcast_to(means[h : h + 1], (8, LANES))
            picked = jnp.take_along_axis(row, low_here, axis=1, mode="promise_in_bounds")
            value = jnp.where(high_here == h, picked, value)
        found.append(value)
    row_means = jnp.concatenate(found, 0)
    curve = hessian[...].astype(jnp.float32)
    adjusted = (gradient[...] + curve * row_means).astype(jnp.bfloat16).astype(jnp.float32)

    level = jnp.max(jnp.abs(adjusted)) * 32.0
    scale, back = jnp.float32(32.0), jnp.float32(1.0 / 32.0)
    for power in (16, 8, 4, 2, 1):
        big = level > 256.0 * 2.0 ** (power - 1)
        level = jnp.where(big, level * 2.0**-power, level)
        scale = jnp.where(big, scale * 2.0**-power, scale)
        back = jnp.where(big, back * 2.0**power, back)
    limit = jnp.sum(curve) * (CROWDED / (LEAVES * BINS))
    is_first = lax.broadcasted_iota(jnp.int32, unscale.shape, 0) == 0
    unscale[...] = jnp.where(is_first, back, limit)

    scaled = adjusted * scale
    adjusted_high = scaled.astype(F8).astype(jnp.float32)
    adjusted_low = (scaled - adjusted_high) * 16.0
    curve_high = curve.astype(F8).astype(jnp.float32)
    curve_low = (curve - curve_high) * 16.0

    half = 2 * LEAVES
    row = lax.broadcasted_iota(jnp.int32, (half, LANES), 0)
    place = row // (2 * share)
    owner = jnp.zeros_like(place)
    for position, other in enumerate(owner_order):
        owner = jnp.where(place == position, other, owner)
    leaf_of = (owner ^ me) * share + (row % (2 * share)) // 2
    leaf_of = leaf_of.astype(jnp.int8)
    is_gradient = (row[:LEAVES] % 2).astype(jnp.int8) == jnp.zeros((), jnp.int8)
    leaves = leaf_ids[...]
    zero = jnp.zeros((), F8)

    def spread(values, j, dtype):
        return jnp.broadcast_to(values[j : j + 1], (LEAVES, LANES)).astype(dtype)

    for j in range(blocks):
        leaf = spread(leaves, j, jnp.int8)
        members = [leaf == leaf_of[:LEAVES], leaf == leaf_of[LEAVES:]]
        parts = []
        for one, two in ((adjusted_high, curve_high), (adjusted_low, curve_low)):
            both = jnp.where(is_gradient, spread(one, j, F8), spread(two, j, F8))
            parts += [jnp.where(member, both, zero) for member in members]
        left[:, j * LANES : (j + 1) * LANES] = jnp.concatenate(parts, 0)


def histogram_kernel(level_step, turned, left, unscale, keep, send, largest):
    step, steps = pl.program_id(0), pl.num_programs(0)
    half = left.shape[0] // 2
    row_count = left.shape[1]
    span = level_step * LANES
    is_gradient = lax.broadcasted_iota(jnp.int32, (half, 1), 0) % 2 == 0
    factor = jnp.where(is_gradient, unscale[0:1, 0:1], 1.0)

    def hot(bins, first_level, dtype):
        one, zero = jnp.ones((), dtype), jnp.zeros((), dtype)
        return jnp.concatenate(
            [jnp.where(bins == (first_level + q).astype(jnp.int8), one, zero) for q in range(level_step)], 1
        )

    def store(step, total):
        where = pl.ds(pl.multiple_of(step * span, span), span)
        keep[:, where] = total[: half // 2]
        send[:, where] = total[half // 2 :]

    both = jnp.dot(
        left[...], hot(turned[...], step * level_step, F8), preferred_element_type=jnp.float32
    )
    total = (both[:half] + both[half:] * 0.0625) * factor
    store(step, total)

    curve = jnp.where(is_gradient, 0.0, total)
    curve = functools.reduce(jnp.maximum, [curve[:, n : n + LANES] for n in range(0, span, LANES)])
    largest[...] = jnp.where(step == 0, curve, jnp.maximum(largest[...], curve))

    @pl.when(step == steps - 1)
    def _():
        crowded = jnp.max(largest[...]) > jnp.max(unscale[1:2])

        @pl.when(crowded)
        def _():
            block = min(1024, row_count)

            def levels(n, nothing):
                def rows(m, total):
                    where = pl.ds(pl.multiple_of(m * block, block), block)
                    weights = left[:half, where].astype(jnp.float32)
                    weights += left[half:, where].astype(jnp.float32) * 0.0625
                    return total + jnp.dot(
                        weights.astype(jnp.bfloat16),
                        hot(turned[where], n * level_step, jnp.bfloat16),
                        preferred_element_type=jnp.float32,
                    )

                total = jnp.zeros((half, span), jnp.float32)
                store(n, lax.fori_loop(0, row_count // block, rows, total) * factor)
                return nothing

            lax.fori_loop(0, steps, levels, 0)


def arrange_kernel(*refs):
    *parts, histograms = refs
    share, features, _ = histograms.shape
    width = features // len(parts)
    copies = LANES // width
    levels = BINS // copies
    for c, own in enumerate(parts):
        for l in range(share):
            rows = []
            for channel in range(2):
                r = 2 * l + channel
                block = jnp.concatenate(
                    [own[r : r + 1, kk * LANES : (kk + 1) * LANES] for kk in range(levels)], 0
                )
                for p in range(copies):
                    rows.append(block if p == 0 else jnp.roll(block, -p * width, axis=1))
            histograms[l, c * width : (c + 1) * width] = jnp.concatenate(rows, 0).T[:width]


def exchange(value, axis, bit):
    count = lax.axis_size(axis)
    return lax.ppermute(value, axis, [(i, i ^ bit) for i in range(count)])


def shards(gradient, hessian, groups, leaf_ids, bins, group_sizes, variance_ratio):
    owners = lax.axis_size("rows")
    bits = [1 << n for n in range(owners.bit_length() - 1)]
    own_groups = group_sizes.shape[0]
    group_count = own_groups * owners
    features, row_count = bins.shape
    blocks = row_count // LANES
    width = features // CHUNKS
    copies = LANES // width
    levels = BINS // copies
    share = LEAVES // owners
    high_count = group_count // LANES
    vmem = pl.BlockSpec(memory_space=pltpu.VMEM)
    smem = pl.BlockSpec(memory_space=pltpu.SMEM)

    gradient = gradient.reshape(blocks, LANES)
    groups = groups.reshape(blocks, LANES)
    leaf_ids = leaf_ids.reshape(blocks, LANES)
    curve = hessian.astype(jnp.float32).reshape(blocks, LANES)

    whole = lambda array: pl.BlockSpec(array.shape, lambda i: (0,) * array.ndim)
    own_rows = own_groups // LANES
    sizes = group_sizes.reshape(own_rows, LANES)
    message = pl.pallas_call(
        group_sum_kernel,
        grid=(1,),
        out_shape=jax.ShapeDtypeStruct((high_count + own_rows, LANES), jnp.float32),
        in_specs=[whole(gradient), whole(groups), whole(sizes)],
        out_specs=vmem,
        compiler_params=STREAM,
        name="group_sum",
    )(gradient, groups, sizes)

    def turn(bins):
        return pl.pallas_call(
            turn_kernel,
            out_shape=jax.ShapeDtypeStruct((row_count, LANES), jnp.int8),
            in_specs=[vmem],
            out_specs=vmem,
            compiler_params=PARAMS,
            cost_estimate=pl.CostEstimate(flops=0, bytes_accessed=4 * bins.size, transcendentals=0),
            name="turn_bins",
        )(bins)

    turned = []
    for n, bit in enumerate(bits):
        other = exchange(message, "rows", bit)
        if n < CHUNKS:
            turned.append(turn(bins[n * width : (n + 1) * width]))
        totals = message[:high_count] + other[:high_count]
        message = jnp.concatenate([totals, message[high_count:], other[high_count:]], 0)
        if n < CHUNKS:
            message, bins, turned = lax.optimization_barrier((message, bins, turned))

    own_total = lax.dynamic_slice_in_dim(message, lax.axis_index("rows") * own_rows, own_rows, 0)
    own_size = message[high_count : high_count + own_rows]
    own_means = (-own_total / (own_size + variance_ratio[0])).reshape(own_groups)

    owner_order = [0]
    for bit in reversed(bits):
        owner_order = owner_order + [o | bit for o in owner_order]
    left, unscale = pl.pallas_call(
        functools.partial(weigh_kernel, owner_order),
        out_shape=(
            jax.ShapeDtypeStruct((4 * LEAVES, row_count), F8),
            jax.ShapeDtypeStruct((8, LANES), jnp.float32),
        ),
        in_specs=[vmem, smem, vmem, vmem, vmem, vmem],
        out_specs=(vmem, vmem),
        compiler_params=PARAMS,
        name="weigh_rows",
    )(message, variance_ratio, gradient, curve, groups, leaf_ids)

    level_step = math.gcd(levels, 4)
    pieces = []
    for part in turned:
        pieces.append(
            pl.pallas_call(
                functools.partial(histogram_kernel, level_step),
                grid=(levels // level_step,),
                out_shape=[jax.ShapeDtypeStruct((LEAVES, levels * LANES), jnp.float32)] * 2,
                in_specs=[whole(part), whole(left), whole(unscale)],
                out_specs=[pl.BlockSpec((LEAVES, levels * LANES), lambda i: (0, 0))] * 2,
                scratch_shapes=[pltpu.VMEM((2 * LEAVES, LANES), jnp.float32)],
                compiler_params=PARAMS,
                cost_estimate=pl.CostEstimate(
                    flops=8 * LEAVES * levels * LANES * row_count, bytes_accessed=0, transcendentals=0
                ),
                name="histogram",
            )(part, left, unscale)
        )
    done = []
    for keep, send in pieces:
        for bit in bits:
            total = keep + exchange(send, "rows", bit)
            middle = total.shape[0] // 2
            keep, send = total[:middle], total[middle:]
        done.append(total)

    histograms = pl.pallas_call(
        arrange_kernel,
        out_shape=jax.ShapeDtypeStruct((share, features, 2 * BINS), jnp.float32),
        in_specs=[vmem] * len(done),
        out_specs=vmem,
        compiler_params=PARAMS,
        name="arrange",
    )(*done)
    return histograms, own_means


def solution(mesh):
    in_specs = (P("rows"), P("rows"), P("rows"), P("rows"), P("feat", "rows"), P("rows"), P())
    out_specs = (P("rows", "feat", None), P("rows"))
    return jax.shard_map(shards, mesh=mesh, in_specs=in_specs, out_specs=out_specs, check_vma=False)
```

```python
import functools
import math

import jax
import jax.numpy as jnp
from jax import lax
from jax.experimental import pallas as pl
from jax.experimental.pallas import tpu as pltpu
from jax.sharding import PartitionSpec as P

BINS = 64
LEAVES = 32
LANES = 128
CHUNKS = 2
CROWDED = 16.0
F8 = jnp.float8_e4m3fn
STREAM = pltpu.CompilerParams(vmem_limit_bytes=60 * 2**20)
PARAMS = pltpu.CompilerParams(vmem_limit_bytes=48 * 2**20)


def group_sum_kernel(gradient, groups, sizes, message):
    blocks = gradient.shape[0]
    own = sizes.shape[0]
    high_count = message.shape[0] - own
    exact = gradient[...]
    first = exact.astype(jnp.bfloat16).astype(jnp.float32)
    rest = exact - first
    second = rest.astype(jnp.bfloat16).astype(jnp.float32)
    parts = (first, second, rest - second)
    ids = groups[...]
    high, low = lax.shift_right_logical(ids, 7), ids & (LANES - 1)
    high_levels = lax.broadcasted_iota(jnp.int32, (high_count, LANES), 0).astype(jnp.int16)
    low_levels = lax.broadcasted_iota(jnp.int32, (LANES, LANES), 0).astype(jnp.int16)
    zero, one = jnp.zeros((), jnp.bfloat16), jnp.ones((), jnp.bfloat16)

    def spread(values, j, rows, dtype):
        return jnp.broadcast_to(values[j : j + 1], (rows, LANES)).astype(dtype)

    total = jnp.zeros((3 * high_count, LANES), jnp.float32)
    step = min(32, blocks)
    for start in range(0, blocks, step):
        left, right = [], []
        for j in range(start, start + step):
            here = spread(high, j, high_count, jnp.int16) == high_levels
            left.append(
                jnp.concatenate(
                    [jnp.where(here, spread(part, j, high_count, jnp.bfloat16), zero) for part in parts],
                    0,
                )
            )
            right.append(jnp.where(spread(low, j, LANES, jnp.int16) == low_levels, one, zero))
        total += lax.dot_general(
            jnp.concatenate(left, 1),
            jnp.concatenate(right, 1),
            (((1,), (1,)), ((), ())),
            preferred_element_type=jnp.float32,
        )
    message[:high_count] = (
        total[:high_count] + (total[high_count : 2 * high_count] + total[2 * high_count :])
    )
    message[high_count:] = sizes[...].astype(jnp.float32)


def turn_kernel(bins, turned):
    features, rows = bins.shape
    copies = LANES // features
    levels = BINS // copies
    for start in range(0, rows, LANES):
        block = bins[:, start : start + LANES]
        stack = jnp.concatenate([block - p * levels for p in range(copies)], 0)
        turned[start : start + LANES] = stack.astype(jnp.int8).T


def weigh_kernel(owner_order, message, ratio, gradient, hessian, groups, leaf_ids, left, unscale):
    blocks = gradient.shape[0]
    high_count = message.shape[0] // 2
    me = lax.axis_index("rows")
    owners = len(owner_order)
    share = LEAVES // owners
    own = high_count // owners
    size_of = jnp.concatenate(
        [message[pl.ds(high_count + (me ^ o) * own, own)] for o in range(owners)], 0
    )
    means = -message[:high_count] / (size_of + ratio[0])
    ids = groups[...]
    high, low = lax.shift_right_logical(ids, 7), ids & (LANES - 1)
    found = []
    for j in range(0, blocks, 8):
        low_here, high_here = low[j : j + 8], high[j : j + 8]
        value = jnp.zeros((8, LANES), jnp.float32)
        for h in range(high_count):
            row = jnp.broadcast_to(means[h : h + 1], (8, LANES))
            picked = jnp.take_along_axis(row, low_here, axis=1, mode="promise_in_bounds")
            value = jnp.where(high_here == h, picked, value)
        found.append(value)
    row_means = jnp.concatenate(found, 0)
    curve = hessian[...].astype(jnp.float32)
    adjusted = (gradient[...] + curve * row_means).astype(jnp.bfloat16).astype(jnp.float32)

    level = jnp.max(jnp.abs(adjusted)) * 32.0
    scale, back = jnp.float32(32.0), jnp.float32(1.0 / 32.0)
    for power in (16, 8, 4, 2, 1):
        big = level > 256.0 * 2.0 ** (power - 1)
        level = jnp.where(big, level * 2.0**-power, level)
        scale = jnp.where(big, scale * 2.0**-power, scale)
        back = jnp.where(big, back * 2.0**power, back)
    limit = jnp.sum(curve) * (CROWDED / (LEAVES * BINS))
    is_first = lax.broadcasted_iota(jnp.int32, unscale.shape, 0) == 0
    unscale[...] = jnp.where(is_first, back, limit)

    scaled = adjusted * scale
    adjusted_high = scaled.astype(F8).astype(jnp.float32)
    adjusted_low = (scaled - adjusted_high) * 16.0
    curve_high = curve.astype(F8).astype(jnp.float32)
    curve_low = (curve - curve_high) * 16.0

    half = 2 * LEAVES
    row = lax.broadcasted_iota(jnp.int32, (half, LANES), 0)
    place = row // (2 * share)
    owner = jnp.zeros_like(place)
    for position, other in enumerate(owner_order):
        owner = jnp.where(place == position, other, owner)
    leaf_of = (owner ^ me) * share + (row % (2 * share)) // 2
    leaf_of = leaf_of.astype(jnp.int8)
    is_gradient = (row[:LEAVES] % 2).astype(jnp.int8) == jnp.zeros((), jnp.int8)
    leaves = leaf_ids[...]
    zero = jnp.zeros((), F8)

    def spread(values, j, dtype):
        return jnp.broadcast_to(values[j : j + 1], (LEAVES, LANES)).astype(dtype)

    for j in range(blocks):
        leaf = spread(leaves, j, jnp.int8)
        members = [leaf == leaf_of[:LEAVES], leaf == leaf_of[LEAVES:]]
        parts = []
        for one, two in ((adjusted_high, curve_high), (adjusted_low, curve_low)):
            both = jnp.where(is_gradient, spread(one, j, F8), spread(two, j, F8))
            parts += [jnp.where(member, both, zero) for member in members]
        left[:, j * LANES : (j + 1) * LANES] = jnp.concatenate(parts, 0)


def histogram_kernel(level_step, turned, left, unscale, keep, send, largest):
    step, steps = pl.program_id(0), pl.num_programs(0)
    half = left.shape[0] // 2
    row_count = left.shape[1]
    span = level_step * LANES
    is_gradient = lax.broadcasted_iota(jnp.int32, (half, 1), 0) % 2 == 0
    factor = jnp.where(is_gradient, unscale[0:1, 0:1], 1.0)

    def hot(bins, first_level, dtype):
        one, zero = jnp.ones((), dtype), jnp.zeros((), dtype)
        return jnp.concatenate(
            [jnp.where(bins == (first_level + q).astype(jnp.int8), one, zero) for q in range(level_step)], 1
        )

    def store(step, total):
        where = pl.ds(pl.multiple_of(step * span, span), span)
        keep[:, where] = total[: half // 2]
        send[:, where] = total[half // 2 :]

    both = jnp.dot(
        left[...], hot(turned[...], step * level_step, F8), preferred_element_type=jnp.float32
    )
    total = (both[:half] + both[half:] * 0.0625) * factor
    store(step, total)

    curve = jnp.where(is_gradient, 0.0, total)
    curve = functools.reduce(jnp.maximum, [curve[:, n : n + LANES] for n in range(0, span, LANES)])
    largest[...] = jnp.where(step == 0, curve, jnp.maximum(largest[...], curve))

    @pl.when(step == steps - 1)
    def _():
        crowded = jnp.max(largest[...] - unscale[1:2]) > 0.0

        @pl.when(crowded)
        def _():
            block = min(1024, row_count)

            def levels(n, nothing):
                def rows(m, total):
                    where = pl.ds(pl.multiple_of(m * block, block), block)
                    weights = left[:half, where].astype(jnp.float32)
                    weights += left[half:, where].astype(jnp.float32) * 0.0625
                    return total + jnp.dot(
                        weights.astype(jnp.bfloat16),
                        hot(turned[where], n * level_step, jnp.bfloat16),
                        preferred_element_type=jnp.float32,
                    )

                total = jnp.zeros((half, span), jnp.float32)
                store(n, lax.fori_loop(0, row_count // block, rows, total) * factor)
                return nothing

            lax.fori_loop(0, steps, levels, 0)


def arrange_kernel(*refs):
    *parts, histograms = refs
    share, features, _ = histograms.shape
    width = features // len(parts)
    copies = LANES // width
    levels = BINS // copies
    for c, own in enumerate(parts):
        for l in range(share):
            rows = []
            for channel in range(2):
                r = 2 * l + channel
                block = jnp.concatenate(
                    [own[r : r + 1, kk * LANES : (kk + 1) * LANES] for kk in range(levels)], 0
                )
                for p in range(copies):
                    rows.append(block if p == 0 else jnp.roll(block, -p * width, axis=1))
            histograms[l, c * width : (c + 1) * width] = jnp.concatenate(rows, 0).T[:width]


def exchange(value, axis, bit):
    count = lax.axis_size(axis)
    return lax.ppermute(value, axis, [(i, i ^ bit) for i in range(count)])


def shards(gradient, hessian, groups, leaf_ids, bins, group_sizes, variance_ratio):
    owners = lax.axis_size("rows")
    bits = [1 << n for n in range(owners.bit_length() - 1)]
    own_groups = group_sizes.shape[0]
    group_count = own_groups * owners
    features, row_count = bins.shape
    blocks = row_count // LANES
    width = features // CHUNKS
    copies = LANES // width
    levels = BINS // copies
    share = LEAVES // owners
    high_count = group_count // LANES
    vmem = pl.BlockSpec(memory_space=pltpu.VMEM)
    smem = pl.BlockSpec(memory_space=pltpu.SMEM)

    gradient = gradient.reshape(blocks, LANES)
    groups = groups.reshape(blocks, LANES)
    leaf_ids = leaf_ids.reshape(blocks, LANES)
    curve = hessian.astype(jnp.float32).reshape(blocks, LANES)

    whole = lambda array: pl.BlockSpec(array.shape, lambda i: (0,) * array.ndim)
    own_rows = own_groups // LANES
    sizes = group_sizes.reshape(own_rows, LANES)
    message = pl.pallas_call(
        group_sum_kernel,
        grid=(1,),
        out_shape=jax.ShapeDtypeStruct((high_count + own_rows, LANES), jnp.float32),
        in_specs=[whole(gradient), whole(groups), whole(sizes)],
        out_specs=vmem,
        compiler_params=STREAM,
        name="group_sum",
    )(gradient, groups, sizes)

    def turn(bins):
        return pl.pallas_call(
            turn_kernel,
            out_shape=jax.ShapeDtypeStruct((row_count, LANES), jnp.int8),
            in_specs=[vmem],
            out_specs=vmem,
            compiler_params=PARAMS,
            cost_estimate=pl.CostEstimate(flops=0, bytes_accessed=4 * bins.size, transcendentals=0),
            name="turn_bins",
        )(bins)

    turned = []
    for n, bit in enumerate(bits):
        other = exchange(message, "rows", bit)
        if n < CHUNKS:
            turned.append(turn(bins[n * width : (n + 1) * width]))
        totals = message[:high_count] + other[:high_count]
        message = jnp.concatenate([totals, message[high_count:], other[high_count:]], 0)
        if n < CHUNKS:
            message, bins, turned = lax.optimization_barrier((message, bins, turned))

    own_total = lax.dynamic_slice_in_dim(message, lax.axis_index("rows") * own_rows, own_rows, 0)
    own_size = message[high_count : high_count + own_rows]
    own_means = (-own_total / (own_size + variance_ratio[0])).reshape(own_groups)

    owner_order = [0]
    for bit in reversed(bits):
        owner_order = owner_order + [o | bit for o in owner_order]
    left, unscale = pl.pallas_call(
        functools.partial(weigh_kernel, owner_order),
        out_shape=(
            jax.ShapeDtypeStruct((4 * LEAVES, row_count), F8),
            jax.ShapeDtypeStruct((8, LANES), jnp.float32),
        ),
        in_specs=[vmem, smem, vmem, vmem, vmem, vmem],
        out_specs=(vmem, vmem),
        compiler_params=PARAMS,
        name="weigh_rows",
    )(message, variance_ratio, gradient, curve, groups, leaf_ids)

    level_step = math.gcd(levels, 8)
    pieces = []
    for part in turned:
        pieces.append(
            pl.pallas_call(
                functools.partial(histogram_kernel, level_step),
                grid=(levels // level_step,),
                out_shape=[jax.ShapeDtypeStruct((LEAVES, levels * LANES), jnp.float32)] * 2,
                in_specs=[whole(part), whole(left), whole(unscale)],
                out_specs=[pl.BlockSpec((LEAVES, levels * LANES), lambda i: (0, 0))] * 2,
                scratch_shapes=[pltpu.VMEM((2 * LEAVES, LANES), jnp.float32)],
                compiler_params=PARAMS,
                cost_estimate=pl.CostEstimate(
                    flops=8 * LEAVES * levels * LANES * row_count, bytes_accessed=0, transcendentals=0
                ),
                name="histogram",
            )(part, left, unscale)
        )
    done = []
    for keep, send in pieces:
        for bit in bits:
            total = keep + exchange(send, "rows", bit)
            middle = total.shape[0] // 2
            keep, send = total[:middle], total[middle:]
        done.append(total)

    histograms = pl.pallas_call(
        arrange_kernel,
        out_shape=jax.ShapeDtypeStruct((share, features, 2 * BINS), jnp.float32),
        in_specs=[vmem] * len(done),
        out_specs=vmem,
        compiler_params=PARAMS,
        name="arrange",
    )(*done)
    return histograms, own_means


def solution(mesh):
    in_specs = (P("rows"), P("rows"), P("rows"), P("rows"), P("feat", "rows"), P("rows"), P())
    out_specs = (P("rows", "feat", None), P("rows"))
    return jax.shard_map(shards, mesh=mesh, in_specs=in_specs, out_specs=out_specs, check_vma=False)
```

```python
import functools
import math

import jax
import jax.numpy as jnp
from jax import lax
from jax.experimental import pallas as pl
from jax.experimental.pallas import tpu as pltpu
from jax.sharding import PartitionSpec as P

BINS = 64
LEAVES = 32
LANES = 128
CHUNKS = 2
CROWDED = 16.0
F8 = jnp.float8_e4m3fn
STREAM = pltpu.CompilerParams(vmem_limit_bytes=60 * 2**20)
PARAMS = pltpu.CompilerParams(vmem_limit_bytes=48 * 2**20)


def group_sum_kernel(gradient, groups, sizes, message):
    blocks = gradient.shape[0]
    own = sizes.shape[0]
    high_count = message.shape[0] - own
    exact = gradient[...]
    first = exact.astype(jnp.bfloat16).astype(jnp.float32)
    rest = exact - first
    second = rest.astype(jnp.bfloat16).astype(jnp.float32)
    parts = (first, second, rest - second)
    ids = groups[...]
    high, low = lax.shift_right_logical(ids, 7), ids & (LANES - 1)
    high_levels = lax.broadcasted_iota(jnp.int32, (high_count, LANES), 0).astype(jnp.int16)
    low_levels = lax.broadcasted_iota(jnp.int32, (LANES, LANES), 0).astype(jnp.int16)
    zero, one = jnp.zeros((), jnp.bfloat16), jnp.ones((), jnp.bfloat16)

    def spread(values, j, rows, dtype):
        return jnp.broadcast_to(values[j : j + 1], (rows, LANES)).astype(dtype)

    total = jnp.zeros((3 * high_count, LANES), jnp.float32)
    step = min(32, blocks)
    for start in range(0, blocks, step):
        left, right = [], []
        for j in range(start, start + step):
            here = spread(high, j, high_count, jnp.int16) == high_levels
            left.append(
                jnp.concatenate(
                    [jnp.where(here, spread(part, j, high_count, jnp.bfloat16), zero) for part in parts],
                    0,
                )
            )
            right.append(jnp.where(spread(low, j, LANES, jnp.int16) == low_levels, one, zero))
        total += lax.dot_general(
            jnp.concatenate(left, 1),
            jnp.concatenate(right, 1),
            (((1,), (1,)), ((), ())),
            preferred_element_type=jnp.float32,
        )
    message[:high_count] = (
        total[:high_count] + (total[high_count : 2 * high_count] + total[2 * high_count :])
    )
    message[high_count:] = sizes[...].astype(jnp.float32)


def turn_kernel(bins, turned):
    features, rows = bins.shape
    copies = LANES // features
    levels = BINS // copies
    for start in range(0, rows, LANES):
        block = bins[:, start : start + LANES]
        stack = jnp.concatenate([block - p * levels for p in range(copies)], 0)
        turned[start : start + LANES] = stack.astype(jnp.int8).T


def weigh_kernel(owner_order, message, ratio, gradient, hessian, groups, leaf_ids, left, unscale):
    blocks = gradient.shape[0]
    high_count = message.shape[0] // 2
    me = lax.axis_index("rows")
    owners = len(owner_order)
    share = LEAVES // owners
    own = high_count // owners
    size_of = jnp.concatenate(
        [message[pl.ds(high_count + (me ^ o) * own, own)] for o in range(owners)], 0
    )
    means = -message[:high_count] / (size_of + ratio[0])
    ids = groups[...]
    high, low = lax.shift_right_logical(ids, 7), ids & (LANES - 1)
    found = []
    for j in range(0, blocks, 8):
        low_here, high_here = low[j : j + 8], high[j : j + 8]
        value = jnp.zeros((8, LANES), jnp.float32)
        for h in range(high_count):
            row = jnp.broadcast_to(means[h : h + 1], (8, LANES))
            picked = jnp.take_along_axis(row, low_here, axis=1, mode="promise_in_bounds")
            value = jnp.where(high_here == h, picked, value)
        found.append(value)
    row_means = jnp.concatenate(found, 0)
    curve = hessian[...].astype(jnp.float32)
    adjusted = (gradient[...] + curve * row_means).astype(jnp.bfloat16).astype(jnp.float32)

    level = jnp.max(jnp.abs(adjusted)) * 32.0
    scale, back = jnp.float32(32.0), jnp.float32(1.0 / 32.0)
    for power in (16, 8, 4, 2, 1):
        big = level > 256.0 * 2.0 ** (power - 1)
        level = jnp.where(big, level * 2.0**-power, level)
        scale = jnp.where(big, scale * 2.0**-power, scale)
        back = jnp.where(big, back * 2.0**power, back)
    limit = jnp.sum(curve) * (CROWDED / (LEAVES * BINS))
    is_first = lax.broadcasted_iota(jnp.int32, unscale.shape, 0) == 0
    unscale[...] = jnp.where(is_first, back, limit)

    scaled = adjusted * scale
    adjusted_high = scaled.astype(F8).astype(jnp.float32)
    adjusted_low = (scaled - adjusted_high) * 16.0
    curve_high = curve.astype(F8).astype(jnp.float32)
    curve_low = (curve - curve_high) * 16.0

    half = 2 * LEAVES
    row = lax.broadcasted_iota(jnp.int32, (half, LANES), 0)
    place = row // (2 * share)
    owner = jnp.zeros_like(place)
    for position, other in enumerate(owner_order):
        owner = jnp.where(place == position, other, owner)
    leaf_of = (owner ^ me) * share + (row % (2 * share)) // 2
    leaf_of = leaf_of.astype(jnp.int8)
    is_gradient = (row[:LEAVES] % 2).astype(jnp.int8) == jnp.zeros((), jnp.int8)
    leaves = leaf_ids[...]
    zero = jnp.zeros((), F8)

    def spread(values, j, dtype):
        return jnp.broadcast_to(values[j : j + 1], (LEAVES, LANES)).astype(dtype)

    for j in range(blocks):
        leaf = spread(leaves, j, jnp.int8)
        members = [leaf == leaf_of[:LEAVES], leaf == leaf_of[LEAVES:]]
        parts = []
        for one, two in ((adjusted_high, curve_high), (adjusted_low, curve_low)):
            both = jnp.where(is_gradient, spread(one, j, F8), spread(two, j, F8))
            parts += [jnp.where(member, both, zero) for member in members]
        left[:, j * LANES : (j + 1) * LANES] = jnp.concatenate(parts, 0)


def histogram_kernel(level_step, turned, left, unscale, keep, send, largest):
    step, steps = pl.program_id(0), pl.num_programs(0)
    half = left.shape[0] // 2
    row_count = left.shape[1]
    span = level_step * LANES
    is_gradient = lax.broadcasted_iota(jnp.int32, (half, 1), 0) % 2 == 0
    factor = jnp.where(is_gradient, unscale[0:1, 0:1], 1.0)

    def hot(bins, first_level, dtype):
        one, zero = jnp.ones((), dtype), jnp.zeros((), dtype)
        return jnp.concatenate(
            [jnp.where(bins == (first_level + q).astype(jnp.int8), one, zero) for q in range(level_step)], 1
        )

    def store(step, total):
        where = pl.ds(pl.multiple_of(step * span, span), span)
        keep[:, where] = total[: half // 2]
        send[:, where] = total[half // 2 :]

    both = jnp.dot(
        left[...], hot(turned[...], step * level_step, F8), preferred_element_type=jnp.float32
    )
    total = (both[:half] + both[half:] * 0.0625) * factor
    store(step, total)

    curve = jnp.where(is_gradient, 0.0, total)
    curve = functools.reduce(jnp.maximum, [curve[:, n : n + LANES] for n in range(0, span, LANES)])
    largest[...] = jnp.where(step == 0, curve, jnp.maximum(largest[...], curve))

    @pl.when(step == steps - 1)
    def _():
        crowded = jnp.max(largest[...] - unscale[1:2]) > 0.0

        @pl.when(crowded)
        def _():
            block = min(1024, row_count)

            def levels(n, nothing):
                def rows(m, total):
                    where = pl.ds(pl.multiple_of(m * block, block), block)
                    weights = left[:half, where].astype(jnp.float32)
                    weights += left[half:, where].astype(jnp.float32) * 0.0625
                    return total + jnp.dot(
                        weights.astype(jnp.bfloat16),
                        hot(turned[where], n * level_step, jnp.bfloat16),
                        preferred_element_type=jnp.float32,
                    )

                total = jnp.zeros((half, span), jnp.float32)
                store(n, lax.fori_loop(0, row_count // block, rows, total) * factor)
                return nothing

            lax.fori_loop(0, steps, levels, 0)


def arrange_kernel(own, *refs):
    histograms = refs[-1]
    share, width, _ = histograms.shape
    copies = LANES // width
    levels = BINS // copies
    for l in range(share):
        rows = []
        for channel in range(2):
            r = 2 * l + channel
            block = jnp.concatenate(
                [own[r : r + 1, kk * LANES : (kk + 1) * LANES] for kk in range(levels)], 0
            )
            for p in range(copies):
                rows.append(block if p == 0 else jnp.roll(block, -p * width, axis=1))
        histograms[l] = jnp.concatenate(rows, 0).T[:width]


def exchange(value, axis, bit):
    count = lax.axis_size(axis)
    return lax.ppermute(value, axis, [(i, i ^ bit) for i in range(count)])


def shards(gradient, hessian, groups, leaf_ids, bins, group_sizes, variance_ratio):
    owners = lax.axis_size("rows")
    bits = [1 << n for n in range(owners.bit_length() - 1)]
    own_groups = group_sizes.shape[0]
    group_count = own_groups * owners
    features, row_count = bins.shape
    blocks = row_count // LANES
    width = features // CHUNKS
    copies = LANES // width
    levels = BINS // copies
    share = LEAVES // owners
    high_count = group_count // LANES
    vmem = pl.BlockSpec(memory_space=pltpu.VMEM)
    smem = pl.BlockSpec(memory_space=pltpu.SMEM)

    gradient = gradient.reshape(blocks, LANES)
    groups = groups.reshape(blocks, LANES)
    leaf_ids = leaf_ids.reshape(blocks, LANES)
    curve = hessian.astype(jnp.float32).reshape(blocks, LANES)

    whole = lambda array: pl.BlockSpec(array.shape, lambda i: (0,) * array.ndim)
    own_rows = own_groups // LANES
    sizes = group_sizes.reshape(own_rows, LANES)
    message = pl.pallas_call(
        group_sum_kernel,
        grid=(1,),
        out_shape=jax.ShapeDtypeStruct((high_count + own_rows, LANES), jnp.float32),
        in_specs=[whole(gradient), whole(groups), whole(sizes)],
        out_specs=vmem,
        compiler_params=STREAM,
        name="group_sum",
    )(gradient, groups, sizes)

    def turn(bins):
        return pl.pallas_call(
            turn_kernel,
            out_shape=jax.ShapeDtypeStruct((row_count, LANES), jnp.int8),
            in_specs=[vmem],
            out_specs=vmem,
            compiler_params=PARAMS,
            cost_estimate=pl.CostEstimate(flops=0, bytes_accessed=4 * bins.size, transcendentals=0),
            name="turn_bins",
        )(bins)

    turned = []
    for n, bit in enumerate(bits):
        other = exchange(message, "rows", bit)
        if n < CHUNKS:
            turned.append(turn(bins[n * width : (n + 1) * width]))
        totals = message[:high_count] + other[:high_count]
        message = jnp.concatenate([totals, message[high_count:], other[high_count:]], 0)
        if n < CHUNKS:
            message, bins, turned = lax.optimization_barrier((message, bins, turned))

    own_total = lax.dynamic_slice_in_dim(message, lax.axis_index("rows") * own_rows, own_rows, 0)
    own_size = message[high_count : high_count + own_rows]
    own_means = (-own_total / (own_size + variance_ratio[0])).reshape(own_groups)

    owner_order = [0]
    for bit in reversed(bits):
        owner_order = owner_order + [o | bit for o in owner_order]
    left, unscale = pl.pallas_call(
        functools.partial(weigh_kernel, owner_order),
        out_shape=(
            jax.ShapeDtypeStruct((4 * LEAVES, row_count), F8),
            jax.ShapeDtypeStruct((8, LANES), jnp.float32),
        ),
        in_specs=[vmem, smem, vmem, vmem, vmem, vmem],
        out_specs=(vmem, vmem),
        compiler_params=PARAMS,
        name="weigh_rows",
    )(message, variance_ratio, gradient, curve, groups, leaf_ids)

    level_step = math.gcd(levels, 16)
    pieces = []
    for part in turned:
        pieces.append(
            pl.pallas_call(
                functools.partial(histogram_kernel, level_step),
                grid=(levels // level_step,),
                out_shape=[jax.ShapeDtypeStruct((LEAVES, levels * LANES), jnp.float32)] * 2,
                in_specs=[whole(part), whole(left), whole(unscale)],
                out_specs=[pl.BlockSpec((LEAVES, levels * LANES), lambda i: (0, 0))] * 2,
                scratch_shapes=[pltpu.VMEM((2 * LEAVES, LANES), jnp.float32)],
                compiler_params=PARAMS,
                cost_estimate=pl.CostEstimate(
                    flops=8 * LEAVES * levels * LANES * row_count, bytes_accessed=0, transcendentals=0
                ),
                name="histogram",
            )(part, left, unscale)
        )
    done = []
    for keep, send in pieces:
        for bit in bits:
            total = keep + exchange(send, "rows", bit)
            middle = total.shape[0] // 2
            keep, send = total[:middle], total[middle:]
        done.append(total)

    histograms = None
    for c, total in enumerate(done):
        before = [] if histograms is None else [histograms]
        histograms = pl.pallas_call(
            arrange_kernel,
            grid=(1,),
            out_shape=jax.ShapeDtypeStruct((share, features, 2 * BINS), jnp.float32),
            in_specs=[whole(total)] + [pl.BlockSpec(memory_space=pl.ANY)] * len(before),
            out_specs=pl.BlockSpec((share, width, 2 * BINS), lambda i, c=c: (0, c, 0)),
            input_output_aliases={1: 0} if before else {},
            compiler_params=PARAMS,
            name="arrange",
        )(total, *before)
    return histograms, own_means


def solution(mesh):
    in_specs = (P("rows"), P("rows"), P("rows"), P("rows"), P("feat", "rows"), P("rows"), P())
    out_specs = (P("rows", "feat", None), P("rows"))
    return jax.shard_map(shards, mesh=mesh, in_specs=in_specs, out_specs=out_specs, check_vma=False)
```
